32 devices in a mesh: expert: 16 (over z, x, core), fsdp: 2 (over y).
Axes of the slice: x: 2, y: 2, z: 4, core: 2. Of those that a mesh axis runs over, the one named last changes fastest.
Arguments:
- tokens: bfloat16 [512, 4096], P('expert', 'fsdp'), may hold values from -6 to 6
- expert_ids: int32 [512, 8], P('expert'), may hold values from 0 to 63, all different within a row; in each aligned block of 32 rows (0 to 31, 32 to 63, ...) at most 8 rows name the same one
- gate_up: bfloat16 [64, 2, 1536, 4096], P('expert', None, 'fsdp'), may hold values from -0.09375 to 0.09375
- hidden_grad: bfloat16 [64, 1536, 128], P('expert', 'fsdp'), may hold values from -1.5 to 1.5
Outputs:
- hidden: bfloat16 [64, 1536, 128], P('expert', 'fsdp')
- gate_up_grad: bfloat16 [64, 2, 1536, 4096], P('expert', None, 'fsdp')
- tokens_grad: bfloat16 [512, 4096], P('expert', 'fsdp')
The draws below stay inside these ranges and needn't reach their ends.
Inputs may be any that keep to these rules, and one draw needn't show every extreme that they name: `expert_ids`: each token names 8 different experts. Among the 32 tokens of each aligned block (the tokens of one expert index) no expert is named by more than 8 tokens, and in some block one expert is named by exactly 8.
All inputs are finite; a program needn't handle non-finite values.
Results may differ from the reference program's by a relative error of at most 0.017.
Values may be sent and summed in bfloat16 or wider, within the bound.
A program may use at most 192 MiB of HBM per device.

```python
import math
import jax
import jax.numpy as jnp
import numpy as np
from jax import lax

D = 4096
FF = 1536
EXPERTS = 64
TOPK = 8
TOK_ROW = 32
CAP = 8
TOKENS = 512
SLOTS = 128
FF_BLOCK = 768
N_EXPERT = 16
N_FSDP = 2


def shard_levels(stream_key, extent, cuts, smallest, top_value):
    loudness = 1.0
    for axis_at, shards_of in cuts:
        draws = jax.random.uniform(jax.random.fold_in(jax.random.fold_in(stream_key, 6), axis_at), (shards_of,), jnp.float32, smallest / len(cuts), top_value / len(cuts))
        loudness = loudness * jnp.repeat(jnp.exp(draws), extent[axis_at] // shards_of).reshape((-1,) + (1,) * (len(extent) - 1 - axis_at))
    return loudness


def deal_out(own_key, own, number, rows, count, top, limit, lean):
    sequence = jax.random.permutation(own_key, count)
    packed, common = portions_of(count, rows * top, limit, lean, True), portions_of(count, rows * top, limit, lean, False)
    places = jnp.arange(count)

    def named(tallies, turn):
        used = int((tallies > 0).sum())
        fixed = max(1, used // 4)
        moved = fixed + (places - fixed + turn * (used - fixed)) % max(1, count - fixed)
        return jnp.zeros((count,), jnp.int32).at[sequence[jnp.where(places < fixed, places, moved)]].set(jnp.asarray(tallies, jnp.int32))

    tallies = jnp.where(number % 4 == 0, named(packed, number // 4), named(common, number - number // 4 - 1))
    mixed = jax.random.permutation(jax.random.fold_in(own, 3), count)
    donor, sink = mixed[0:count // 2 * 2:2], mixed[1:count // 2 * 2:2]
    slack = jnp.minimum(tallies[donor] - 1, limit - tallies[sink]) // 2
    slack = jnp.where((donor == sequence[0]) | (sink == sequence[0]) | (tallies[sink] == 0), 0, jnp.maximum(slack, 0))
    moved = jax.random.randint(jax.random.fold_in(own, 4), (count // 2,), 0, 1 << 20) % (slack + 1)
    tallies = tallies.at[donor].add(-moved).at[sink].add(moved)
    items = jnp.searchsorted(jnp.cumsum(tallies), jnp.arange(rows * top), side="right").astype(jnp.int32)
    listing = items.reshape(top, rows).T
    listing = listing[jax.random.permutation(jax.random.fold_in(own, 1), rows)]
    turn = jax.random.randint(jax.random.fold_in(own, 2), (rows, 1), 0, top)
    return jnp.take_along_axis(listing, (jnp.arange(top)[None, :] + turn) % top, axis=1)


def portions_of(count, total, limit, skew, full):
    loads = [(1 << 20) // math.isqrt(rank ** skew) + 1 for rank in range(1, count + 1)]
    largest = limit if full else min(limit, max(-(-total // count), total * loads[0] // sum(loads)))
    least = 1 if total - largest >= count - 1 else 0
    counts, rest = [largest] + [least] * (count - 1), total - largest - least * (count - 1)
    while rest > 0:
        movable = [i for i in range(1, count) if counts[i] < largest] or [i for i in range(1, count) if counts[i] < limit]
        mass, budget = sum([loads[i] for i in movable]), rest
        for i in movable:
            more = min(limit - counts[i], max(1, budget * loads[i] // mass), rest)
            counts[i] = counts[i] + more
            rest = rest - more
    return np.array(counts)


def gaussian(rng, dims, scale, reach, cuts=(), kind=jnp.bfloat16):
    loudness = shard_levels(rng, dims, cuts, -0.22, 0.18) if cuts else 1.0
    result = jax.random.normal(rng, dims, jnp.float32) * scale * loudness
    return jnp.minimum(jnp.maximum(result, -reach), reach).astype(kind)


def setup_inputs(seed: int = 0) -> dict:
    seeds = jax.random.split(jax.random.key(seed), 5)
    tokens = gaussian(seeds[0], (TOKENS, D), 1.0, 6.0, ((0, 16), (1, 2)))
    expert_ids_keys = jax.random.split(jax.random.fold_in(seeds[1], 1), TOKENS // TOK_ROW)
    expert_ids_turns = jax.random.permutation(jax.random.fold_in(seeds[1], 3), TOKENS // TOK_ROW)
    expert_ids = jax.vmap(lambda own, number: deal_out(jax.random.fold_in(seeds[1], 2), own, number, TOK_ROW, EXPERTS, TOPK, CAP, 2))(expert_ids_keys, expert_ids_turns).reshape((TOKENS, TOPK))
    gate_up = gaussian(seeds[2], (EXPERTS, 2, FF, D), D ** -0.5, 0.09375, ((0, 16), (2, 2)))
    hidden_grad = gaussian(seeds[3], (EXPERTS, FF, SLOTS), 0.25, 1.5, ((0, 16), (1, 2)))
    return {"tokens": tokens, "expert_ids": expert_ids, "gate_up": gate_up, "hidden_grad": hidden_grad}


def slot_layout(expert_ids):
    blocks = expert_ids.astype(jnp.int32).reshape(N_EXPERT, TOK_ROW, TOPK)
    expert_iota = jnp.arange(EXPERTS, dtype=jnp.int32)
    chosen = jnp.sum((blocks[:, :, :, None] == expert_iota).astype(jnp.int32), axis=2)
    before = jnp.cumsum(chosen, axis=1) - chosen
    slot_iota = jnp.arange(CAP, dtype=jnp.int32)
    placed = (chosen[:, :, :, None] == 1) & (before[:, :, :, None] == slot_iota)
    return placed.astype(jnp.float32)


def expert_pass(items):
    routed_x, weights, grad_hidden = items
    gate_value = jnp.dot(weights[0], routed_x.T, preferred_element_type=jnp.float32)
    up_value = jnp.dot(weights[1], routed_x.T, preferred_element_type=jnp.float32)
    sigmoid_gate = 1.0 / (1.0 + jnp.exp(-gate_value))
    active = gate_value * sigmoid_gate
    hidden = (active * up_value).astype(jnp.bfloat16)
    grad_value = grad_hidden.astype(jnp.float32)
    gate_grad = (grad_value * up_value * sigmoid_gate * (1.0 + gate_value * (1.0 - sigmoid_gate))).astype(jnp.bfloat16)
    up_grad = (grad_value * active).astype(jnp.bfloat16)
    weight_grad = jnp.stack([
        jnp.dot(gate_grad, routed_x, preferred_element_type=jnp.float32),
        jnp.dot(up_grad, routed_x, preferred_element_type=jnp.float32),
    ]).astype(jnp.bfloat16)
    block_grads = jnp.stack([gate_grad, up_grad]).astype(jnp.float32).reshape(2, N_FSDP, FF_BLOCK, SLOTS)
    block_weights = weights.astype(jnp.float32).reshape(2, N_FSDP, FF_BLOCK, D)
    parts = jnp.einsum("wqis,wqid->qsd", block_grads, block_weights, precision=lax.Precision.HIGHEST)
    parts = lax.optimization_barrier(parts.astype(jnp.bfloat16)).astype(jnp.float32)
    return hidden, weight_grad, jnp.sum(parts, axis=0)


def reference(tokens, expert_ids, gate_up, hidden_grad):
    placed = slot_layout(expert_ids)
    blocks = tokens.astype(jnp.float32).reshape(N_EXPERT, TOK_ROW, D)
    routed = jnp.einsum("btxc,btd->xbcd", placed, blocks, precision=lax.Precision.HIGHEST)
    routed = routed.reshape(EXPERTS, SLOTS, D).astype(jnp.bfloat16)
    hidden, weight_grad, slot_total = lax.map(expert_pass, (routed, gate_up, hidden_grad))
    slot_total = slot_total.reshape(EXPERTS, N_EXPERT, CAP, D)
    token_grad = jnp.einsum("btxc,xbcd->btd", placed, slot_total, precision=lax.Precision.HIGHEST)
    return hidden, weight_grad, token_grad.reshape(TOKENS, D).astype(jnp.bfloat16)
```

```python
import jax
import jax.numpy as jnp
from jax import lax
from jax.sharding import PartitionSpec as P


def selector_of(ids, first, local_experts, groups, capacity):
    rows = ids.shape[0] // groups
    mine = first + jnp.arange(local_experts, dtype=jnp.int32)
    chosen = jnp.sum((ids[:, :, None] == mine).astype(jnp.int32), axis=1)
    chosen = chosen.reshape(groups, rows, local_experts)
    before = jnp.cumsum(chosen, axis=1) - chosen
    group = jnp.arange(groups, dtype=jnp.int32)[:, None, None]
    slot = jnp.where(chosen == 1, group * capacity + before, -1)
    slot = slot.reshape(groups * rows, local_experts)
    slots = jnp.arange(groups * capacity, dtype=jnp.int32)
    return (slot.T[:, None, :] == slots[None, :, None]).astype(jnp.bfloat16)


def local(tokens, expert_ids, gate_up, hidden_grad):
    groups = lax.axis_size("expert")
    local_experts, _, units, model_width = gate_up.shape
    slot_count = hidden_grad.shape[2]
    capacity = slot_count // groups
    ids = lax.all_gather(expert_ids, "expert", axis=0, tiled=True)
    selector = selector_of(
        ids, lax.axis_index("expert") * local_experts, local_experts, groups, capacity
    )
    features = lax.all_gather(tokens, "fsdp", axis=1, tiled=True)
    features = lax.all_gather(features, "expert", axis=0, tiled=True)
    routed = jnp.einsum(
        "jst,td->jsd", selector, features, preferred_element_type=jnp.float32
    ).astype(jnp.bfloat16)
    projected = jnp.einsum("jwid,jsd->jwis", gate_up, routed, preferred_element_type=jnp.float32)
    gate_value = projected[:, 0]
    up_value = projected[:, 1]
    sigmoid_gate = 1.0 / (1.0 + jnp.exp(-gate_value))
    active = gate_value * sigmoid_gate
    hidden = (active * up_value).astype(jnp.bfloat16)
    grad_value = hidden_grad.astype(jnp.float32)
    gate_grad = (
        grad_value * up_value * sigmoid_gate * (1.0 + gate_value * (1.0 - sigmoid_gate))
    ).astype(jnp.bfloat16)
    up_grad = (grad_value * active).astype(jnp.bfloat16)
    grad_pair = jnp.stack([gate_grad, up_grad], axis=1)
    part = jnp.einsum(
        "jwis,jwid->jsd", grad_pair, gate_up, preferred_element_type=jnp.float32
    ).astype(jnp.bfloat16)
    partial = jnp.einsum(
        "jst,jsd->td", selector, part, preferred_element_type=jnp.float32
    ).astype(jnp.bfloat16)
    summed = lax.psum_scatter(partial, "expert", scatter_dimension=0, tiled=True)
    token_grad = lax.psum_scatter(summed, "fsdp", scatter_dimension=1, tiled=True)
    weight_grad = jnp.einsum(
        "jwis,jsd->jwid", grad_pair, routed, preferred_element_type=jnp.float32
    ).astype(jnp.bfloat16)
    return (hidden, weight_grad, token_grad)


def solution(mesh):
    placed = (
        P("expert", "fsdp"),
        P("expert", None),
        P("expert", None, "fsdp", None),
        P("expert", "fsdp", None),
    )
    return jax.shard_map(
        local,
        mesh=mesh,
        in_specs=placed,
        out_specs=(P("expert", "fsdp", None), P("expert", None, "fsdp", None), P("expert", "fsdp")),
        check_vma=False,
    )
```

```python
import functools

import jax
import jax.numpy as jnp
from jax import lax
from jax.experimental import pallas as pl
from jax.experimental.pallas import tpu as pltpu
from jax.sharding import PartitionSpec as P

MIB = 2**20
MESH = pl.DeviceIdType.MESH


class Place:
    def __init__(self, groups):
        self.depth = groups // 4
        index = lax.axis_index("expert")
        self.core = lax.rem(index, 2)
        self.x = lax.rem(lax.div(index, 2), 2)
        self.z = lax.div(index, 4)
        self.y = lax.axis_index("fsdp")

    def along(self, step):
        return lax.rem(self.z + step + self.depth, self.depth)

    def expert(self, z, x, core):
        return (z * 2 + x) * 2 + core

    def device(self, z=None, x=None, y=None, core=None):
        z = self.z if z is None else z
        x = self.x if x is None else x
        core = self.core if core is None else core
        return (self.expert(z, x, core), self.y if y is None else y)

    def greet(self):
        barrier = pltpu.get_barrier_semaphore()
        peers = [self.device(z=self.along(k)) for k in range(1, self.depth)]
        peers += [self.device(x=1 - self.x), self.device(y=1 - self.y)]
        peers += [self.device(core=1 - self.core)]
        for peer in peers:
            pl.semaphore_signal(barrier, inc=1, device_id=peer, device_id_type=MESH)
        pl.semaphore_wait(barrier, len(peers))


def remote(source, target, sends, recvs, at, device):
    copy = pltpu.make_async_remote_copy(
        src_ref=source,
        dst_ref=target,
        send_sem=sends.at[at],
        recv_sem=recvs.at[at],
        device_id=device,
        device_id_type=MESH,
    )
    return copy


def gather_kernel(groups, own, full, z_send, z_recv, p_send, p_recv, q_send, q_recv, c_send, c_recv, own_sem):
    me = Place(groups)
    depth = me.depth
    me.greet()
    other = me.device(core=1 - me.core)
    partner = [me.device(x=1 - me.x), me.device(y=1 - me.y)]
    started = []

    def slab(h, k, kind):
        far_x = kind in ((1, 3) if h == 0 else (2, 3))
        far_y = kind in ((2, 3) if h == 0 else (1, 3))
        x = 1 - me.x if far_x else me.x
        y = 1 - me.y if far_y else me.y
        return full.at[y, me.expert(me.along(-k), x, me.core), h]

    def hand_on(h, k, kind, source):
        target = slab(h, k, kind)
        first, second = (partner[0], partner[1]) if h == 0 else (partner[1], partner[0])
        copies = []
        if kind == 0:
            copies.append(remote(source, target, p_send, p_recv, (h, k), first))
        if kind in (0, 1):
            copies.append(remote(source, target, q_send, q_recv, (h, k, kind), second))
        copies.append(remote(source, target, c_send, c_recv, (h, k, kind), other))
        for copy in copies:
            copy.start()
            started.append(copy)

    def arrived(sems, at, h, k, kind):
        target = slab(h, k, kind)
        remote(target, target, sems, sems, at, other).wait_recv()

    mine = pltpu.make_async_copy(own, full.at[me.y, lax.axis_index("expert")], own_sem)
    mine.start()
    for k in range(1, depth):
        for h in range(2):
            copy = remote(
                own.at[h], slab(h, 0, 0), z_send, z_recv, (h, k), me.device(z=me.along(k))
            )
            copy.start()
            started.append(copy)
    for h in range(2):
        hand_on(h, 0, 0, own.at[h])
    for k in range(depth):
        if k > 0:
            for h in range(2):
                arrived(z_recv, (h, k), h, k, 0)
                hand_on(h, k, 0, slab(h, k, 0))
        for h in range(2):
            arrived(p_recv, (h, k), h, k, 1)
            hand_on(h, k, 1, slab(h, k, 1))
    for k in range(depth):
        for kind in (2, 3):
            for h in range(2):
                arrived(q_recv, (h, k, kind - 2), h, k, kind)
                hand_on(h, k, kind, slab(h, k, kind))
    for k in range(depth):
        for kind in range(4):
            for h in range(2):
                far = full.at[me.y, me.expert(me.along(-k), me.x, 1 - me.core), h]
                remote(far, far, c_send, c_recv, (h, k, kind), other).wait_recv()
    for copy in started:
        copy.wait_send()
    mine.wait()


def gather_tokens(own, groups, fsdp):
    depth = groups // 4
    dma = pltpu.SemaphoreType.DMA
    return pl.pallas_call(
        functools.partial(gather_kernel, groups),
        out_shape=jax.ShapeDtypeStruct((fsdp, groups) + own.shape, own.dtype),
        in_specs=[pl.BlockSpec(memory_space=pl.ANY)],
        out_specs=pl.BlockSpec(memory_space=pl.ANY),
        scratch_shapes=[
            dma((2, depth)),
            dma((2, depth)),
            dma((2, depth)),
            dma((2, depth)),
            dma((2, depth, 2)),
            dma((2, depth, 2)),
            dma((2, depth, 4)),
            dma((2, depth, 4)),
            dma,
        ],
        compiler_params=pltpu.CompilerParams(collective_id=0, has_side_effects=True),
        name="gather_tokens",
    )(own)


def add_into(target, term):
    total = target[...].astype(jnp.float32) + term[...].astype(jnp.float32)
    target[...] = total.astype(target.dtype)


def scatter_kernel(groups, part, out, one, two, three, four, s1, r1, s2, r2, s3, r3, s4, r4):
    me = Place(groups)
    depth = me.depth
    me.greet()
    other = me.device(core=1 - me.core)
    x_peer, y_peer = me.device(x=1 - me.x), me.device(y=1 - me.y)
    started = []
    order = list(range(1, depth)) + [0]

    def send(*what):
        copy = remote(*what)
        copy.start()
        started.append(copy)

    def arrived(target, sems, at):
        remote(target, target, sems, sems, at, other).wait_recv()

    def side(i, mine):
        return 1 - mine if i == 0 else mine

    for k in order:
        for i, j in ((0, 0), (0, 1), (1, 0), (1, 1)):
            block = me.expert(me.along(k), side(j, me.x), 1 - me.core)
            source = part.at[side(i, me.y), block]
            send(source, one.at[k, i, j], s1, r1, (k, i, j), other)
    for k in order:
        for i, j in ((0, 0), (0, 1), (1, 0), (1, 1)):
            arrived(one.at[k, i, j], r1, (k, i, j))
            block = me.expert(me.along(k), side(j, me.x), me.core)
            add_into(one.at[k, i, j], part.at[side(i, me.y), block])
            if i == 0:
                send(one.at[k, 0, j, 0], two.at[0, k, j], s2, r2, (0, k, j), y_peer)
            if j == 0:
                send(one.at[k, i, 0, 1], two.at[1, k, i], s2, r2, (1, k, i), x_peer)
    for k in order:
        for j in range(2):
            arrived(two.at[0, k, j], r2, (0, k, j))
            add_into(two.at[0, k, j], one.at[k, 1, j, 0])
            arrived(two.at[1, k, j], r2, (1, k, j))
            add_into(two.at[1, k, j], one.at[k, j, 1, 1])
            if j == 0:
                send(two.at[0, k, 0], three.at[0, k], s3, r3, (0, k), x_peer)
                send(two.at[1, k, 0], three.at[1, k], s3, r3, (1, k), y_peer)
    for k in order:
        for h in range(2):
            arrived(three.at[h, k], r3, (h, k))
            add_into(three.at[h, k], two.at[h, k, 1])
            if k > 0:
                send(three.at[h, k], four.at[h, k], s4, r4, (h, k), me.device(z=me.along(k)))
    for h in range(2):
        total = three[h, 0].astype(jnp.float32)
        for k in range(1, depth):
            arrived(four.at[h, k], r4, (h, k))
            total = total + four[h, k].astype(jnp.float32)
        out[h] = total.astype(out.dtype)
    for copy in started:
        copy.wait_send()


def scatter_sum(part):
    _, groups, halves, rows, width = part.shape
    depth = groups // 4
    dma = pltpu.SemaphoreType.DMA
    vmem = lambda *lead: pltpu.VMEM(lead + (rows, width), part.dtype)
    return pl.pallas_call(
        functools.partial(scatter_kernel, groups),
        out_shape=jax.ShapeDtypeStruct((halves, rows, width), part.dtype),
        in_specs=[pl.BlockSpec(memory_space=pltpu.VMEM)],
        out_specs=pl.BlockSpec(memory_space=pltpu.VMEM),
        scratch_shapes=[
            vmem(depth, 2, 2, 2),
            vmem(2, depth, 2),
            vmem(2, depth),
            vmem(2, depth),
            dma((depth, 2, 2)),
            dma((depth, 2, 2)),
            dma((2, depth, 2)),
            dma((2, depth, 2)),
            dma((2, depth)),
            dma((2, depth)),
            dma((2, depth)),
            dma((2, depth)),
        ],
        compiler_params=pltpu.CompilerParams(
            collective_id=1, has_side_effects=True, vmem_limit_bytes=24 * MIB
        ),
        name="scatter_sum",
    )(part)


def mixed_kernel(
    features, chosen, chosen_back, weights, grad, hidden, weight_grad, summed, routed, parts, pair, turned
):
    expert, turn = pl.program_id(0), pl.program_id(1)
    sides, _, half = features.shape
    units, slots = pair.shape[1:]
    width = routed.shape[1]
    half_width = summed.shape[2]
    tile = 512 if half_width % 512 == 0 else 128
    rows = 256 if units % 256 == 0 else 16
    f32 = jnp.float32

    @pl.when(turn == 0)
    def _():
        @pl.loop(0, half_width // tile)
        def _(n):
            at = pl.ds(pl.multiple_of(n * tile, tile), tile)
            for side in range(sides):
                to = pl.ds(pl.multiple_of(side * half_width + n * tile, tile), tile)
                routed[:, to] = jnp.dot(
                    chosen[0], features[side, :, at], preferred_element_type=f32
                ).astype(routed.dtype)

        @pl.loop(0, units // rows)
        def _(n):
            at = pl.ds(pl.multiple_of(n * rows, rows), rows)
            contract = (((1,), (1,)), ((), ()))
            gate = lax.dot_general(
                weights[0, 0, at, :], routed[...], contract, preferred_element_type=f32
            )
            up = lax.dot_general(
                weights[0, 1, at, :], routed[...], contract, preferred_element_type=f32
            )
            sigmoid = 1.0 / (1.0 + jnp.exp(-gate))
            active = gate * sigmoid
            hidden[0, at, :] = (active * up).astype(hidden.dtype)
            slope = grad[0, at, :].astype(f32)
            pair[0, at, :] = (slope * up * sigmoid * (1.0 + gate * (1.0 - sigmoid))).astype(pair.dtype)
            pair[1, at, :] = (slope * active).astype(pair.dtype)

    @pl.loop(0, width // tile)
    def _(n):
        at = pl.ds(pl.multiple_of(n * tile, tile), tile)
        weight_grad[0, 0, :, at] = jnp.dot(
            pair[turn], routed[:, at], preferred_element_type=f32
        ).astype(weight_grad.dtype)

    @pl.when(turn == 1)
    def _():
        turned[0] = pair[0].T
        turned[1] = pair[1].T

        @pl.loop(0, width // tile)
        def _(n):
            at = pl.ds(pl.multiple_of(n * tile, tile), tile)
            total = jnp.dot(turned[0], weights[0, 0, :, at], preferred_element_type=f32)
            total += jnp.dot(turned[1], weights[0, 1, :, at], preferred_element_type=f32)
            parts[pl.ds(pl.multiple_of(expert * slots, slots), slots), at] = total.astype(parts.dtype)

    @pl.when((turn == 1) & (expert == pl.num_programs(0) - 1))
    def _():
        @pl.loop(0, half_width // tile)
        def _(n):
            at = pl.ds(pl.multiple_of(n * tile, tile), tile)
            for side in range(sides):
                come = pl.ds(pl.multiple_of(side * half_width + n * tile, tile), tile)
                summed[side, :, at] = jnp.dot(
                    chosen_back[...], parts[:, come], preferred_element_type=f32
                ).astype(summed.dtype)


def mixed(features, selector, gate_up, hidden_grad, half_width):
    experts, _, units, width = gate_up.shape
    slots = hidden_grad.shape[2]
    sides, tokens, _ = features.shape
    back = jnp.transpose(selector.reshape(experts * slots, tokens))
    bf16 = gate_up.dtype
    flops = 2 * experts * units * width * slots * 6
    whole = pl.BlockSpec(memory_space=pltpu.VMEM)
    return pl.pallas_call(
        mixed_kernel,
        grid=(experts, 2),
        out_shape=(
            jax.ShapeDtypeStruct(hidden_grad.shape, bf16),
            jax.ShapeDtypeStruct(gate_up.shape, bf16),
            jax.ShapeDtypeStruct((sides, tokens, half_width), bf16),
        ),
        in_specs=[
            whole,
            pl.BlockSpec((1, slots, tokens), lambda j, p: (j, 0, 0)),
            whole,
            pl.BlockSpec((1, 2, units, width), lambda j, p: (j, 0, 0, 0)),
            pl.BlockSpec((1, units, slots), lambda j, p: (j, 0, 0)),
        ],
        out_specs=(
            pl.BlockSpec((1, units, slots), lambda j, p: (j, 0, 0)),
            pl.BlockSpec((1, 1, units, width), lambda j, p: (j, p, 0, 0)),
            whole,
        ),
        scratch_shapes=[
            pltpu.VMEM((slots, width), bf16),
            pltpu.VMEM((experts * slots, width), bf16),
            pltpu.VMEM((2, units, slots), bf16),
            pltpu.VMEM((2, slots, units), bf16),
        ],
        compiler_params=pltpu.CompilerParams(
            dimension_semantics=("arbitrary", "arbitrary"), vmem_limit_bytes=60 * MIB
        ),
        cost_estimate=pl.CostEstimate(
            flops=flops, bytes_accessed=4 * gate_up.size, transcendentals=experts * units * slots
        ),
        name="expert_pass",
    )(features, selector, back, gate_up, hidden_grad)


def selector_of(ids, first, local_experts, groups, capacity):
    rows = ids.shape[0] // groups
    mine = first + jnp.arange(local_experts, dtype=jnp.int32)
    chosen = jnp.sum((ids[:, :, None] == mine).astype(jnp.int32), axis=1)
    chosen = chosen.reshape(groups, rows, local_experts)
    before = jnp.cumsum(chosen, axis=1) - chosen
    group = jnp.arange(groups, dtype=jnp.int32)[:, None, None]
    slot = jnp.where(chosen == 1, group * capacity + before, -1)
    slot = slot.reshape(groups * rows, local_experts)
    slots = jnp.arange(groups * capacity, dtype=jnp.int32)
    return (slot.T[:, None, :] == slots[None, :, None]).astype(jnp.bfloat16)


def local_plain(tokens, expert_ids, gate_up, hidden_grad):
    groups = lax.axis_size("expert")
    local_experts, _, units, model_width = gate_up.shape
    slot_count = hidden_grad.shape[2]
    capacity = slot_count // groups
    ids = lax.all_gather(expert_ids, "expert", axis=0, tiled=True)
    selector = selector_of(
        ids, lax.axis_index("expert") * local_experts, local_experts, groups, capacity
    )
    features = lax.all_gather(tokens, "fsdp", axis=1, tiled=True)
    features = lax.all_gather(features, "expert", axis=0, tiled=True)
    routed = jnp.einsum(
        "jst,td->jsd", selector, features, preferred_element_type=jnp.float32
    ).astype(jnp.bfloat16)
    projected = jnp.einsum("jwid,jsd->jwis", gate_up, routed, preferred_element_type=jnp.float32)
    gate_value = projected[:, 0]
    up_value = projected[:, 1]
    sigmoid_gate = 1.0 / (1.0 + jnp.exp(-gate_value))
    active = gate_value * sigmoid_gate
    hidden = (active * up_value).astype(jnp.bfloat16)
    grad_value = hidden_grad.astype(jnp.float32)
    gate_grad = (
        grad_value * up_value * sigmoid_gate * (1.0 + gate_value * (1.0 - sigmoid_gate))
    ).astype(jnp.bfloat16)
    up_grad = (grad_value * active).astype(jnp.bfloat16)
    grad_pair = jnp.stack([gate_grad, up_grad], axis=1)
    part = jnp.einsum(
        "jwis,jwid->jsd", grad_pair, gate_up, preferred_element_type=jnp.float32
    ).astype(jnp.bfloat16)
    partial = jnp.einsum(
        "jst,jsd->td", selector, part, preferred_element_type=jnp.float32
    ).astype(jnp.bfloat16)
    summed = lax.psum_scatter(partial, "expert", scatter_dimension=0, tiled=True)
    token_grad = lax.psum_scatter(summed, "fsdp", scatter_dimension=1, tiled=True)
    weight_grad = jnp.einsum(
        "jwis,jsd->jwid", grad_pair, routed, preferred_element_type=jnp.float32
    ).astype(jnp.bfloat16)
    return (hidden, weight_grad, token_grad)


def local(tokens, expert_ids, gate_up, hidden_grad):
    groups, fsdp = lax.axis_size("expert"), lax.axis_size("fsdp")
    local_experts = gate_up.shape[0]
    capacity = hidden_grad.shape[2] // groups
    rows, width = tokens.shape
    listing = jnp.pad(expert_ids.astype(tokens.dtype), ((0, 0), (0, 128 - expert_ids.shape[1])))
    own = jnp.concatenate([tokens, listing], axis=1).reshape(2, rows // 2, width + 128)
    full = gather_tokens(own, groups, fsdp).reshape(fsdp, groups * rows, width + 128)
    ids = full[0, :, width : width + expert_ids.shape[1]].astype(jnp.int32)
    selector = selector_of(
        ids, lax.axis_index("expert") * local_experts, local_experts, groups, capacity
    )
    hidden, weight_grad, partial = mixed(full, selector, gate_up, hidden_grad, width)
    token_grad = scatter_sum(partial.reshape(fsdp, groups, 2, rows // 2, width))
    return (hidden, weight_grad, token_grad.reshape(rows, width))


def fits(mesh, gate_up_shape, ids_shape, tokens_shape):
    groups, fsdp = mesh.shape["expert"], mesh.shape["fsdp"]
    rows = tokens_shape[0] // groups
    return (
        groups % 4 == 0
        and fsdp == 2
        and rows % 32 == 0
        and (tokens_shape[1] // fsdp) % 128 == 0
        and gate_up_shape[0] <= 256
        and ids_shape[1] <= 128
    )


def solution(mesh):
    placed = (
        P("expert", "fsdp"),
        P("expert", None),
        P("expert", None, "fsdp", None),
        P("expert", "fsdp", None),
    )
    results = (P("expert", "fsdp", None), P("expert", None, "fsdp", None), P("expert", "fsdp"))

    def run(tokens, expert_ids, gate_up, hidden_grad):
        kernels = fits(mesh, gate_up.shape, expert_ids.shape, tokens.shape)
        return jax.shard_map(
            local if kernels else local_plain,
            mesh=mesh,
            in_specs=placed,
            out_specs=results,
            check_vma=False,
        )(tokens, expert_ids, gate_up, hidden_grad)

    return run
```

```python
import functools

import jax
import jax.numpy as jnp
from jax import lax
from jax.experimental import pallas as pl
from jax.experimental.pallas import tpu as pltpu
from jax.sharding import PartitionSpec as P

MIB = 2**20
MESH = pl.DeviceIdType.MESH


class Place:
    def __init__(self, groups):
        self.depth = groups // 4
        index = lax.axis_index("expert")
        self.core = lax.rem(index, 2)
        self.x = lax.rem(lax.div(index, 2), 2)
        self.z = lax.div(index, 4)
        self.y = lax.axis_index("fsdp")

    def along(self, step):
        return lax.rem(self.z + step + self.depth, self.depth)

    def expert(self, z, x, core):
        return (z * 2 + x) * 2 + core

    def device(self, z=None, x=None, y=None, core=None):
        z = self.z if z is None else z
        x = self.x if x is None else x
        core = self.core if core is None else core
        return (self.expert(z, x, core), self.y if y is None else y)

    def greet(self):
        barrier = pltpu.get_barrier_semaphore()
        peers = [self.device(z=self.along(k)) for k in range(1, self.depth)]
        peers += [self.device(x=1 - self.x), self.device(y=1 - self.y)]
        peers += [self.device(core=1 - self.core)]
        for peer in peers:
            pl.semaphore_signal(barrier, inc=1, device_id=peer, device_id_type=MESH)
        pl.semaphore_wait(barrier, len(peers))


def remote(source, target, sends, recvs, at, device):
    copy = pltpu.make_async_remote_copy(
        src_ref=source,
        dst_ref=target,
        send_sem=sends.at[at],
        recv_sem=recvs.at[at],
        device_id=device,
        device_id_type=MESH,
    )
    return copy


def gather_kernel(groups, own, full, z_send, z_recv, p_send, p_recv, q_send, q_recv, c_send, c_recv, own_sem):
    me = Place(groups)
    depth = me.depth
    me.greet()
    other = me.device(core=1 - me.core)
    partner = [me.device(x=1 - me.x), me.device(y=1 - me.y)]
    started = []

    def slab(h, k, kind):
        far_x = kind in ((1, 3) if h == 0 else (2, 3))
        far_y = kind in ((2, 3) if h == 0 else (1, 3))
        x = 1 - me.x if far_x else me.x
        y = 1 - me.y if far_y else me.y
        return full.at[y, me.expert(me.along(-k), x, me.core), h]

    def hand_on(h, k, kind, source):
        target = slab(h, k, kind)
        first, second = (partner[0], partner[1]) if h == 0 else (partner[1], partner[0])
        copies = []
        if kind == 0:
            copies.append(remote(source, target, p_send, p_recv, (h, k), first))
        if kind in (0, 1):
            copies.append(remote(source, target, q_send, q_recv, (h, k, kind), second))
        copies.append(remote(source, target, c_send, c_recv, (h, k, kind), other))
        for copy in copies:
            copy.start()
            started.append(copy)

    def arrived(sems, at, h, k, kind):
        target = slab(h, k, kind)
        remote(target, target, sems, sems, at, other).wait_recv()

    mine = pltpu.make_async_copy(own, full.at[me.y, lax.axis_index("expert")], own_sem)
    mine.start()
    for k in range(1, depth):
        for h in range(2):
            copy = remote(
                own.at[h], slab(h, 0, 0), z_send, z_recv, (h, k), me.device(z=me.along(k))
            )
            copy.start()
            started.append(copy)
    for h in range(2):
        hand_on(h, 0, 0, own.at[h])
    for k in range(depth):
        if k > 0:
            for h in range(2):
                arrived(z_recv, (h, k), h, k, 0)
                hand_on(h, k, 0, slab(h, k, 0))
        for h in range(2):
            arrived(p_recv, (h, k), h, k, 1)
            hand_on(h, k, 1, slab(h, k, 1))
    for k in range(depth):
        for kind in (2, 3):
            for h in range(2):
                arrived(q_recv, (h, k, kind - 2), h, k, kind)
                hand_on(h, k, kind, slab(h, k, kind))
    for k in range(depth):
        for kind in range(4):
            for h in range(2):
                far = full.at[me.y, me.expert(me.along(-k), me.x, 1 - me.core), h]
                remote(far, far, c_send, c_recv, (h, k, kind), other).wait_recv()
    for copy in started:
        copy.wait_send()
    mine.wait()


def gather_tokens(own, groups, fsdp):
    depth = groups // 4
    dma = pltpu.SemaphoreType.DMA
    return pl.pallas_call(
        functools.partial(gather_kernel, groups),
        out_shape=jax.ShapeDtypeStruct((fsdp, groups) + own.shape, own.dtype),
        in_specs=[pl.BlockSpec(memory_space=pl.ANY)],
        out_specs=pl.BlockSpec(memory_space=pl.ANY),
        scratch_shapes=[
            dma((2, depth)),
            dma((2, depth)),
            dma((2, depth)),
            dma((2, depth)),
            dma((2, depth, 2)),
            dma((2, depth, 2)),
            dma((2, depth, 4)),
            dma((2, depth, 4)),
            dma,
        ],
        compiler_params=pltpu.CompilerParams(collective_id=0, has_side_effects=True),
        name="gather_tokens",
    )(own)


def add_into(target, term):
    total = target[...].astype(jnp.float32) + term[...].astype(jnp.float32)
    target[...] = total.astype(target.dtype)


def scatter_kernel(
    groups, rows, turned, back, weights, out, part, rowgrad, held, one, two, three, four,
    load, s1, r1, s2, r2, s3, r3, s4, r4,
):
    me = Place(groups)
    depth = me.depth
    experts, _, slots, _ = turned.shape
    chunks, sides, _, width = part.shape
    half_width = chunks * width
    half = rows // 2
    tile = 512 if width % 512 == 0 else 128
    halves = [pl.ds(0, half), pl.ds(half, half)]
    f32 = jnp.float32

    def fetch(step):
        chunk, expert = divmod(step, experts)
        slot = step % 2
        return [
            pltpu.make_async_copy(
                weights.at[expert, :, :, pl.ds(side * half_width + chunk * width, width)],
                held.at[slot, side],
                load.at[slot, side],
            )
            for side in range(sides)
        ]

    for copy in fetch(0):
        copy.start()
    me.greet()
    other = me.device(core=1 - me.core)
    x_peer, y_peer = me.device(x=1 - me.x), me.device(y=1 - me.y)
    started = []
    order = list(range(1, depth)) + [0]

    def send(*what):
        copy = remote(*what)
        copy.start()
        started.append(copy)

    def arrived(target, sems, at):
        remote(target, target, sems, sems, at, other).wait_recv()

    def side_of(i, mine):
        return 1 - mine if i == 0 else mine

    def block(c, k, i, j, core):
        expert = me.expert(me.along(k), side_of(j, me.x), core)
        at = pl.ds(pl.multiple_of(expert * rows, rows), rows)
        return part.at[c, side_of(i, me.y), at]

    corners = ((0, 0), (0, 1), (1, 0), (1, 1))

    def to_core(c):
        for k in order:
            for i, j in corners:
                source = block(c, k, i, j, 1 - me.core)
                send(source, one.at[c, k, i, j], s1, r1, (c, k, i, j), other)

    def to_first(c):
        for k in order:
            for i, j in corners:
                arrived(one.at[c, k, i, j], r1, (c, k, i, j))
                add_into(one.at[c, k, i, j], block(c, k, i, j, me.core))
                if i == 0:
                    source = one.at[c, k, 0, j, halves[0]]
                    send(source, two.at[c, 0, k, j], s2, r2, (c, 0, k, j), y_peer)
                if j == 0:
                    source = one.at[c, k, i, 0, halves[1]]
                    send(source, two.at[c, 1, k, i], s2, r2, (c, 1, k, i), x_peer)

    def to_second(c):
        for k in order:
            for j in range(2):
                arrived(two.at[c, 0, k, j], r2, (c, 0, k, j))
                add_into(two.at[c, 0, k, j], one.at[c, k, 1, j, halves[0]])
                arrived(two.at[c, 1, k, j], r2, (c, 1, k, j))
                add_into(two.at[c, 1, k, j], one.at[c, k, j, 1, halves[1]])
                if j == 0:
                    send(two.at[c, 0, k, 0], three.at[c, 0, k], s3, r3, (c, 0, k), x_peer)
                    send(two.at[c, 1, k, 0], three.at[c, 1, k], s3, r3, (c, 1, k), y_peer)

    def to_owner(c):
        for k in order:
            for h in range(2):
                arrived(three.at[c, h, k], r3, (c, h, k))
                add_into(three.at[c, h, k], two.at[c, h, k, 1])
                if k > 0:
                    owner = me.device(z=me.along(k))
                    send(three.at[c, h, k], four.at[c, h, k], s4, r4, (c, h, k), owner)

    def finish(c):
        for h in range(2):
            total = three[c, h, 0].astype(f32)
            for k in range(1, depth):
                arrived(four.at[c, h, k], r4, (c, h, k))
                total = total + four[c, h, k].astype(f32)
            out[halves[h], pl.ds(c * width, width)] = total.astype(out.dtype)

    stages = [to_first, to_second, to_owner, finish]
    waiting = []
    for step in range(chunks * experts):
        chunk, expert = divmod(step, experts)
        slot = step % 2
        if step + 1 < chunks * experts:
            for copy in fetch(step + 1):
                copy.start()
        for copy in fetch(step):
            copy.wait()
        for side in range(sides):

            @pl.loop(0, width // tile)
            def _(n):
                at = pl.ds(pl.multiple_of(n * tile, tile), tile)
                total = jnp.dot(
                    turned[expert, 0], held[slot, side, 0, :, at], preferred_element_type=f32
                )
                total += jnp.dot(
                    turned[expert, 1], held[slot, side, 1, :, at], preferred_element_type=f32
                )
                rowgrad[side, pl.ds(expert * slots, slots), at] = total.astype(rowgrad.dtype)

            if waiting:
                waiting.pop(0)()
        if expert == experts - 1:
            for side in range(sides):

                @pl.loop(0, width // tile)
                def _(n):
                    at = pl.ds(pl.multiple_of(n * tile, tile), tile)
                    part[chunk, side, :, at] = jnp.dot(
                        back[...], rowgrad[side, :, at], preferred_element_type=f32
                    ).astype(part.dtype)

            to_core(chunk)
            waiting += [functools.partial(stage, chunk) for stage in stages]
    for stage in waiting:
        stage()
    for copy in started:
        copy.wait_send()


def scatter_sum(turned, selector, gate_up, groups, rows, half_width, sides):
    experts, _, units, _ = gate_up.shape
    slots, tokens = selector.shape[1:]
    depth = groups // 4
    chunks = 2 if half_width % 256 == 0 else 1
    width = half_width // chunks
    bf16 = gate_up.dtype
    back = jnp.transpose(selector.reshape(experts * slots, tokens))
    dma = pltpu.SemaphoreType.DMA
    vmem = lambda *dims: pltpu.VMEM(dims + (width,), bf16)
    whole = pl.BlockSpec(memory_space=pltpu.VMEM)
    return pl.pallas_call(
        functools.partial(scatter_kernel, groups, rows),
        out_shape=jax.ShapeDtypeStruct((rows, half_width), bf16),
        in_specs=[whole, whole, pl.BlockSpec(memory_space=pl.ANY)],
        out_specs=whole,
        scratch_shapes=[
            vmem(chunks, sides, tokens),
            vmem(sides, experts * slots),
            vmem(2, sides, 2, units),
            vmem(chunks, depth, 2, 2, rows),
            vmem(chunks, 2, depth, 2, rows // 2),
            vmem(chunks, 2, depth, rows // 2),
            vmem(chunks, 2, depth, rows // 2),
            dma((2, sides)),
            dma((chunks, depth, 2, 2)),
            dma((chunks, depth, 2, 2)),
            dma((chunks, 2, depth, 2)),
            dma((chunks, 2, depth, 2)),
            dma((chunks, 2, depth)),
            dma((chunks, 2, depth)),
            dma((chunks, 2, depth)),
            dma((chunks, 2, depth)),
        ],
        compiler_params=pltpu.CompilerParams(
            collective_id=1, has_side_effects=True, vmem_limit_bytes=58 * MIB
        ),
        cost_estimate=pl.CostEstimate(
            flops=2 * gate_up.size * slots, bytes_accessed=2 * gate_up.size, transcendentals=0
        ),
        name="row_gradient",
    )(turned, back, gate_up)


def mixed_kernel(
    features, chosen, weights, grad, hidden, weight_grad, turned, routed, pair
):
    turn = pl.program_id(1)
    sides = features.shape[0]
    units = pair.shape[1]
    width = routed.shape[1]
    half_width = width // sides
    tile = 512 if half_width % 512 == 0 else 128
    rows = 256 if units % 256 == 0 else 16
    f32 = jnp.float32

    @pl.when(turn == 0)
    def _():
        @pl.loop(0, half_width // tile)
        def _(n):
            at = pl.ds(pl.multiple_of(n * tile, tile), tile)
            for side in range(sides):
                to = pl.ds(pl.multiple_of(side * half_width + n * tile, tile), tile)
                routed[:, to] = jnp.dot(
                    chosen[0], features[side, :, at], preferred_element_type=f32
                ).astype(routed.dtype)

        @pl.loop(0, units // rows)
        def _(n):
            at = pl.ds(pl.multiple_of(n * rows, rows), rows)
            contract = (((1,), (1,)), ((), ()))
            gate = lax.dot_general(
                weights[0, 0, at, :], routed[...], contract, preferred_element_type=f32
            )
            up = lax.dot_general(
                weights[0, 1, at, :], routed[...], contract, preferred_element_type=f32
            )
            sigmoid = 1.0 / (1.0 + jnp.exp(-gate))
            active = gate * sigmoid
            hidden[0, at, :] = (active * up).astype(hidden.dtype)
            slope = grad[0, at, :].astype(f32)
            pair[0, at, :] = (slope * up * sigmoid * (1.0 + gate * (1.0 - sigmoid))).astype(pair.dtype)
            pair[1, at, :] = (slope * active).astype(pair.dtype)

    @pl.loop(0, width // tile)
    def _(n):
        at = pl.ds(pl.multiple_of(n * tile, tile), tile)
        weight_grad[0, 0, :, at] = jnp.dot(
            pair[turn], routed[:, at], preferred_element_type=f32
        ).astype(weight_grad.dtype)

    @pl.when(turn == 0)
    def _():
        turned[0, 0] = pair[0].T
        turned[0, 1] = pair[1].T


def mixed(features, selector, gate_up, hidden_grad):
    experts, _, units, width = gate_up.shape
    slots = hidden_grad.shape[2]
    sides, tokens, _ = features.shape
    bf16 = gate_up.dtype
    flops = 2 * experts * units * width * slots * 4
    whole = pl.BlockSpec(memory_space=pltpu.VMEM)
    return pl.pallas_call(
        mixed_kernel,
        grid=(experts, 2),
        out_shape=(
            jax.ShapeDtypeStruct(hidden_grad.shape, bf16),
            jax.ShapeDtypeStruct(gate_up.shape, bf16),
            jax.ShapeDtypeStruct((experts, 2, slots, units), bf16),
        ),
        in_specs=[
            whole,
            pl.BlockSpec((1, slots, tokens), lambda j, p: (j, 0, 0)),
            pl.BlockSpec((1, 2, units, width), lambda j, p: (j, 0, 0, 0)),
            pl.BlockSpec((1, units, slots), lambda j, p: (j, 0, 0)),
        ],
        out_specs=(
            pl.BlockSpec((1, units, slots), lambda j, p: (j, 0, 0)),
            pl.BlockSpec((1, 1, units, width), lambda j, p: (j, p, 0, 0)),
            pl.BlockSpec((1, 2, slots, units), lambda j, p: (j, 0, 0, 0)),
        ),
        scratch_shapes=[
            pltpu.VMEM((slots, width), bf16),
            pltpu.VMEM((2, units, slots), bf16),
        ],
        compiler_params=pltpu.CompilerParams(
            dimension_semantics=("arbitrary", "arbitrary"), vmem_limit_bytes=60 * MIB
        ),
        cost_estimate=pl.CostEstimate(
            flops=flops, bytes_accessed=4 * gate_up.size, transcendentals=experts * units * slots
        ),
        name="expert_pass",
    )(features, selector, gate_up, hidden_grad)


def selector_of(ids, first, local_experts, groups, capacity):
    rows = ids.shape[0] // groups
    mine = first + jnp.arange(local_experts, dtype=jnp.int32)
    chosen = jnp.sum((ids[:, :, None] == mine).astype(jnp.int32), axis=1)
    chosen = chosen.reshape(groups, rows, local_experts)
    before = jnp.cumsum(chosen, axis=1) - chosen
    group = jnp.arange(groups, dtype=jnp.int32)[:, None, None]
    slot = jnp.where(chosen == 1, group * capacity + before, -1)
    slot = slot.reshape(groups * rows, local_experts)
    slots = jnp.arange(groups * capacity, dtype=jnp.int32)
    return (slot.T[:, None, :] == slots[None, :, None]).astype(jnp.bfloat16)


def local_plain(tokens, expert_ids, gate_up, hidden_grad):
    groups = lax.axis_size("expert")
    local_experts, _, units, model_width = gate_up.shape
    slot_count = hidden_grad.shape[2]
    capacity = slot_count // groups
    ids = lax.all_gather(expert_ids, "expert", axis=0, tiled=True)
    selector = selector_of(
        ids, lax.axis_index("expert") * local_experts, local_experts, groups, capacity
    )
    features = lax.all_gather(tokens, "fsdp", axis=1, tiled=True)
    features = lax.all_gather(features, "expert", axis=0, tiled=True)
    routed = jnp.einsum(
        "jst,td->jsd", selector, features, preferred_element_type=jnp.float32
    ).astype(jnp.bfloat16)
    projected = jnp.einsum("jwid,jsd->jwis", gate_up, routed, preferred_element_type=jnp.float32)
    gate_value = projected[:, 0]
    up_value = projected[:, 1]
    sigmoid_gate = 1.0 / (1.0 + jnp.exp(-gate_value))
    active = gate_value * sigmoid_gate
    hidden = (active * up_value).astype(jnp.bfloat16)
    grad_value = hidden_grad.astype(jnp.float32)
    gate_grad = (
        grad_value * up_value * sigmoid_gate * (1.0 + gate_value * (1.0 - sigmoid_gate))
    ).astype(jnp.bfloat16)
    up_grad = (grad_value * active).astype(jnp.bfloat16)
    grad_pair = jnp.stack([gate_grad, up_grad], axis=1)
    part = jnp.einsum(
        "jwis,jwid->jsd", grad_pair, gate_up, preferred_element_type=jnp.float32
    ).astype(jnp.bfloat16)
    partial = jnp.einsum(
        "jst,jsd->td", selector, part, preferred_element_type=jnp.float32
    ).astype(jnp.bfloat16)
    summed = lax.psum_scatter(partial, "expert", scatter_dimension=0, tiled=True)
    token_grad = lax.psum_scatter(summed, "fsdp", scatter_dimension=1, tiled=True)
    weight_grad = jnp.einsum(
        "jwis,jsd->jwid", grad_pair, routed, preferred_element_type=jnp.float32
    ).astype(jnp.bfloat16)
    return (hidden, weight_grad, token_grad)


def local(tokens, expert_ids, gate_up, hidden_grad):
    groups, fsdp = lax.axis_size("expert"), lax.axis_size("fsdp")
    local_experts = gate_up.shape[0]
    capacity = hidden_grad.shape[2] // groups
    rows, width = tokens.shape
    listing = jnp.pad(expert_ids.astype(tokens.dtype), ((0, 0), (0, 128 - expert_ids.shape[1])))
    own = jnp.concatenate([tokens, listing], axis=1).reshape(2, rows // 2, width + 128)
    full = gather_tokens(own, groups, fsdp).reshape(fsdp, groups * rows, width + 128)
    ids = full[0, :, width : width + expert_ids.shape[1]].astype(jnp.int32)
    selector = selector_of(
        ids, lax.axis_index("expert") * local_experts, local_experts, groups, capacity
    )
    hidden, weight_grad, turned = mixed(full, selector, gate_up, hidden_grad)
    token_grad = scatter_sum(turned, selector, gate_up, groups, rows, width, fsdp)
    return (hidden, weight_grad, token_grad)


def fits(mesh, gate_up_shape, ids_shape, tokens_shape):
    groups, fsdp = mesh.shape["expert"], mesh.shape["fsdp"]
    rows = tokens_shape[0] // groups
    return (
        groups % 4 == 0
        and fsdp == 2
        and rows % 32 == 0
        and (tokens_shape[1] // fsdp) % 128 == 0
        and gate_up_shape[0] <= 256
        and ids_shape[1] <= 128
    )


def solution(mesh):
    placed = (
        P("expert", "fsdp"),
        P("expert", None),
        P("expert", None, "fsdp", None),
        P("expert", "fsdp", None),
    )
    results = (P("expert", "fsdp", None), P("expert", None, "fsdp", None), P("expert", "fsdp"))

    def run(tokens, expert_ids, gate_up, hidden_grad):
        kernels = fits(mesh, gate_up.shape, expert_ids.shape, tokens.shape)
        return jax.shard_map(
            local if kernels else local_plain,
            mesh=mesh,
            in_specs=placed,
            out_specs=results,
            check_vma=False,
        )(tokens, expert_ids, gate_up, hidden_grad)

    return run
```

```python
import functools

import jax
import jax.numpy as jnp
from jax import lax
from jax.experimental import pallas as pl
from jax.experimental.pallas import tpu as pltpu
from jax.sharding import PartitionSpec as P

MIB = 2**20
MESH = pl.DeviceIdType.MESH


class Place:
    def __init__(self, groups):
        self.depth = groups // 4
        index = lax.axis_index("expert")
        self.core = lax.rem(index, 2)
        self.x = lax.rem(lax.div(index, 2), 2)
        self.z = lax.div(index, 4)
        self.y = lax.axis_index("fsdp")

    def along(self, step):
        return lax.rem(self.z + step + self.depth, self.depth)

    def expert(self, z, x, core):
        return (z * 2 + x) * 2 + core

    def device(self, z=None, x=None, y=None, core=None):
        z = self.z if z is None else z
        x = self.x if x is None else x
        core = self.core if core is None else core
        return (self.expert(z, x, core), self.y if y is None else y)

    def greet(self):
        barrier = pltpu.get_barrier_semaphore()
        peers = [self.device(z=self.along(k)) for k in range(1, self.depth)]
        peers += [self.device(x=1 - self.x), self.device(y=1 - self.y)]
        peers += [self.device(core=1 - self.core)]
        for peer in peers:
            pl.semaphore_signal(barrier, inc=1, device_id=peer, device_id_type=MESH)
        pl.semaphore_wait(barrier, len(peers))


def remote(source, target, sends, recvs, at, device):
    copy = pltpu.make_async_remote_copy(
        src_ref=source,
        dst_ref=target,
        send_sem=sends.at[at],
        recv_sem=recvs.at[at],
        device_id=device,
        device_id_type=MESH,
    )
    return copy


def gather_kernel(groups, own, full, z_send, z_recv, p_send, p_recv, q_send, q_recv, c_send, c_recv, own_sem):
    me = Place(groups)
    depth = me.depth
    me.greet()
    other = me.device(core=1 - me.core)
    partner = [me.device(x=1 - me.x), me.device(y=1 - me.y)]
    started = []

    def slab(h, k, kind):
        far_x = kind in ((1, 3) if h == 0 else (2, 3))
        far_y = kind in ((2, 3) if h == 0 else (1, 3))
        x = 1 - me.x if far_x else me.x
        y = 1 - me.y if far_y else me.y
        return full.at[y, me.expert(me.along(-k), x, me.core), h]

    def hand_on(h, k, kind, source):
        target = slab(h, k, kind)
        first, second = (partner[0], partner[1]) if h == 0 else (partner[1], partner[0])
        copies = []
        if kind == 0:
            copies.append(remote(source, target, p_send, p_recv, (h, k), first))
        if kind in (0, 1):
            copies.append(remote(source, target, q_send, q_recv, (h, k, kind), second))
        copies.append(remote(source, target, c_send, c_recv, (h, k, kind), other))
        for copy in copies:
            copy.start()
            started.append(copy)

    def arrived(sems, at, h, k, kind):
        target = slab(h, k, kind)
        remote(target, target, sems, sems, at, other).wait_recv()

    mine = pltpu.make_async_copy(own, full.at[me.y, lax.axis_index("expert")], own_sem)
    mine.start()
    for k in range(1, depth):
        for h in range(2):
            copy = remote(
                own.at[h], slab(h, 0, 0), z_send, z_recv, (h, k), me.device(z=me.along(k))
            )
            copy.start()
            started.append(copy)
    for h in range(2):
        hand_on(h, 0, 0, own.at[h])
    for k in range(depth):
        if k > 0:
            for h in range(2):
                arrived(z_recv, (h, k), h, k, 0)
                hand_on(h, k, 0, slab(h, k, 0))
        for h in range(2):
            arrived(p_recv, (h, k), h, k, 1)
            hand_on(h, k, 1, slab(h, k, 1))
    for k in range(depth):
        for kind in (2, 3):
            for h in range(2):
                arrived(q_recv, (h, k, kind - 2), h, k, kind)
                hand_on(h, k, kind, slab(h, k, kind))
    for k in range(depth):
        for kind in range(4):
            for h in range(2):
                far = full.at[me.y, me.expert(me.along(-k), me.x, 1 - me.core), h]
                remote(far, far, c_send, c_recv, (h, k, kind), other).wait_recv()
    for copy in started:
        copy.wait_send()
    mine.wait()


def gather_tokens(own, groups, fsdp):
    depth = groups // 4
    dma = pltpu.SemaphoreType.DMA
    return pl.pallas_call(
        functools.partial(gather_kernel, groups),
        out_shape=jax.ShapeDtypeStruct((fsdp, groups) + own.shape, own.dtype),
        in_specs=[pl.BlockSpec(memory_space=pl.ANY)],
        out_specs=pl.BlockSpec(memory_space=pl.ANY),
        scratch_shapes=[
            dma((2, depth)),
            dma((2, depth)),
            dma((2, depth)),
            dma((2, depth)),
            dma((2, depth, 2)),
            dma((2, depth, 2)),
            dma((2, depth, 4)),
            dma((2, depth, 4)),
            dma,
        ],
        compiler_params=pltpu.CompilerParams(collective_id=0, has_side_effects=True),
        name="gather_tokens",
    )(own)


def add_into(target, term):
    total = target[...].astype(jnp.float32) + term[...].astype(jnp.float32)
    target[...] = total.astype(target.dtype)


def scatter_kernel(groups, part, out, one, two, three, four, s1, r1, s2, r2, s3, r3, s4, r4):
    me = Place(groups)
    depth = me.depth
    me.greet()
    other = me.device(core=1 - me.core)
    x_peer, y_peer = me.device(x=1 - me.x), me.device(y=1 - me.y)
    started = []
    order = list(range(1, depth)) + [0]

    def send(*what):
        copy = remote(*what)
        copy.start()
        started.append(copy)

    def arrived(target, sems, at):
        remote(target, target, sems, sems, at, other).wait_recv()

    def side(i, mine):
        return 1 - mine if i == 0 else mine

    for k in order:
        for i, j in ((0, 0), (0, 1), (1, 0), (1, 1)):
            block = me.expert(me.along(k), side(j, me.x), 1 - me.core)
            source = part.at[side(i, me.y), block]
            send(source, one.at[k, i, j], s1, r1, (k, i, j), other)
    for k in order:
        for i, j in ((0, 0), (0, 1), (1, 0), (1, 1)):
            arrived(one.at[k, i, j], r1, (k, i, j))
            block = me.expert(me.along(k), side(j, me.x), me.core)
            add_into(one.at[k, i, j], part.at[side(i, me.y), block])
            if i == 0:
                send(one.at[k, 0, j, 0], two.at[0, k, j], s2, r2, (0, k, j), y_peer)
            if j == 0:
                send(one.at[k, i, 0, 1], two.at[1, k, i], s2, r2, (1, k, i), x_peer)
    for k in order:
        for j in range(2):
            arrived(two.at[0, k, j], r2, (0, k, j))
            add_into(two.at[0, k, j], one.at[k, 1, j, 0])
            arrived(two.at[1, k, j], r2, (1, k, j))
            add_into(two.at[1, k, j], one.at[k, j, 1, 1])
            if j == 0:
                send(two.at[0, k, 0], three.at[0, k], s3, r3, (0, k), x_peer)
                send(two.at[1, k, 0], three.at[1, k], s3, r3, (1, k), y_peer)
    for k in order:
        for h in range(2):
            arrived(three.at[h, k], r3, (h, k))
            add_into(three.at[h, k], two.at[h, k, 1])
            if k > 0:
                send(three.at[h, k], four.at[h, k], s4, r4, (h, k), me.device(z=me.along(k)))
    for h in range(2):
        total = three[h, 0].astype(jnp.float32)
        for k in range(1, depth):
            arrived(four.at[h, k], r4, (h, k))
            total = total + four[h, k].astype(jnp.float32)
        out[h] = total.astype(out.dtype)
    for copy in started:
        copy.wait_send()


def scatter_sum(part):
    _, groups, halves, rows, width = part.shape
    depth = groups // 4
    dma = pltpu.SemaphoreType.DMA
    vmem = lambda *lead: pltpu.VMEM(lead + (rows, width), part.dtype)
    return pl.pallas_call(
        functools.partial(scatter_kernel, groups),
        out_shape=jax.ShapeDtypeStruct((halves, rows, width), part.dtype),
        in_specs=[pl.BlockSpec(memory_space=pltpu.VMEM)],
        out_specs=pl.BlockSpec(memory_space=pltpu.VMEM),
        scratch_shapes=[
            vmem(depth, 2, 2, 2),
            vmem(2, depth, 2),
            vmem(2, depth),
            vmem(2, depth),
            dma((depth, 2, 2)),
            dma((depth, 2, 2)),
            dma((2, depth, 2)),
            dma((2, depth, 2)),
            dma((2, depth)),
            dma((2, depth)),
            dma((2, depth)),
            dma((2, depth)),
        ],
        compiler_params=pltpu.CompilerParams(
            collective_id=1, has_side_effects=True, vmem_limit_bytes=24 * MIB
        ),
        name="scatter_sum",
    )(part)


def mixed_kernel(
    features, chosen, chosen_back, weights, grad, hidden, weight_grad, summed, routed, parts, pair, total
):
    expert, turn = pl.program_id(0), pl.program_id(1)
    last = pl.num_programs(1) - 1
    sides = features.shape[0]
    slots, width = routed.shape
    half_width = summed.shape[2]
    tile = 512 if half_width % 512 == 0 else 128
    f32 = jnp.float32

    @pl.when(turn == 0)
    def _():
        @pl.loop(0, half_width // tile)
        def _(n):
            at = pl.ds(pl.multiple_of(n * tile, tile), tile)
            for side in range(sides):
                to = pl.ds(pl.multiple_of(side * half_width + n * tile, tile), tile)
                routed[:, to] = jnp.dot(
                    chosen[0], features[side, :, at], preferred_element_type=f32
                ).astype(routed.dtype)

        total[...] = jnp.zeros_like(total)

    contract = (((1,), (1,)), ((), ()))
    gate = lax.dot_general(weights[0, 0], routed[...], contract, preferred_element_type=f32)
    up = lax.dot_general(weights[0, 1], routed[...], contract, preferred_element_type=f32)
    sigmoid = 1.0 / (1.0 + jnp.exp(-gate))
    active = gate * sigmoid
    hidden[0] = (active * up).astype(hidden.dtype)
    slope = grad[0].astype(f32)
    pair[0] = (slope * up * sigmoid * (1.0 + gate * (1.0 - sigmoid))).astype(pair.dtype)
    pair[1] = (slope * active).astype(pair.dtype)
    turned = [pair[0].T, pair[1].T]

    @pl.loop(0, width // tile)
    def _(n):
        at = pl.ds(pl.multiple_of(n * tile, tile), tile)
        for w in range(2):
            weight_grad[0, w, :, at] = jnp.dot(
                pair[w], routed[:, at], preferred_element_type=f32
            ).astype(weight_grad.dtype)
        rows = jnp.dot(turned[0], weights[0, 0, :, at], preferred_element_type=f32)
        rows += jnp.dot(turned[1], weights[0, 1, :, at], preferred_element_type=f32)
        total[:, at] += rows

    @pl.when(turn == last)
    def _():
        at = pl.ds(pl.multiple_of(expert * slots, slots), slots)
        parts[at, :] = total[...].astype(parts.dtype)

    @pl.when((turn == last) & (expert == pl.num_programs(0) - 1))
    def _():
        @pl.loop(0, half_width // tile)
        def _(n):
            at = pl.ds(pl.multiple_of(n * tile, tile), tile)
            for side in range(sides):
                come = pl.ds(pl.multiple_of(side * half_width + n * tile, tile), tile)
                summed[side, :, at] = jnp.dot(
                    chosen_back[...], parts[:, come], preferred_element_type=f32
                ).astype(summed.dtype)


def mixed(features, selector, gate_up, hidden_grad, half_width):
    experts, _, units, width = gate_up.shape
    slots = hidden_grad.shape[2]
    sides, tokens, _ = features.shape
    back = jnp.transpose(selector.reshape(experts * slots, tokens))
    bf16 = gate_up.dtype
    rows = 256 if units % 256 == 0 else 16
    flops = 2 * experts * units * width * slots * 6
    whole = pl.BlockSpec(memory_space=pltpu.VMEM)
    return pl.pallas_call(
        mixed_kernel,
        grid=(experts, units // rows),
        out_shape=(
            jax.ShapeDtypeStruct(hidden_grad.shape, bf16),
            jax.ShapeDtypeStruct(gate_up.shape, bf16),
            jax.ShapeDtypeStruct((sides, tokens, half_width), bf16),
        ),
        in_specs=[
            whole,
            pl.BlockSpec((1, slots, tokens), lambda j, p: (j, 0, 0)),
            whole,
            pl.BlockSpec((1, 2, rows, width), lambda j, p: (j, 0, p, 0)),
            pl.BlockSpec((1, rows, slots), lambda j, p: (j, p, 0)),
        ],
        out_specs=(
            pl.BlockSpec((1, rows, slots), lambda j, p: (j, p, 0)),
            pl.BlockSpec((1, 2, rows, width), lambda j, p: (j, 0, p, 0)),
            whole,
        ),
        scratch_shapes=[
            pltpu.VMEM((slots, width), bf16),
            pltpu.VMEM((experts * slots, width), bf16),
            pltpu.VMEM((2, rows, slots), bf16),
            pltpu.VMEM((slots, width), jnp.float32),
        ],
        compiler_params=pltpu.CompilerParams(
            dimension_semantics=("arbitrary", "arbitrary"), vmem_limit_bytes=60 * MIB
        ),
        cost_estimate=pl.CostEstimate(
            flops=flops, bytes_accessed=4 * gate_up.size, transcendentals=experts * units * slots
        ),
        name="expert_pass",
    )(features, selector, back, gate_up, hidden_grad)


def selector_of(ids, first, local_experts, groups, capacity):
    rows = ids.shape[0] // groups
    mine = first + jnp.arange(local_experts, dtype=jnp.int32)
    chosen = jnp.sum((ids[:, :, None] == mine).astype(jnp.int32), axis=1)
    chosen = chosen.reshape(groups, rows, local_experts)
    before = jnp.cumsum(chosen, axis=1) - chosen
    group = jnp.arange(groups, dtype=jnp.int32)[:, None, None]
    slot = jnp.where(chosen == 1, group * capacity + before, -1)
    slot = slot.reshape(groups * rows, local_experts)
    slots = jnp.arange(groups * capacity, dtype=jnp.int32)
    return (slot.T[:, None, :] == slots[None, :, None]).astype(jnp.bfloat16)


def local_plain(tokens, expert_ids, gate_up, hidden_grad):
    groups = lax.axis_size("expert")
    local_experts, _, units, model_width = gate_up.shape
    slot_count = hidden_grad.shape[2]
    capacity = slot_count // groups
    ids = lax.all_gather(expert_ids, "expert", axis=0, tiled=True)
    selector = selector_of(
        ids, lax.axis_index("expert") * local_experts, local_experts, groups, capacity
    )
    features = lax.all_gather(tokens, "fsdp", axis=1, tiled=True)
    features = lax.all_gather(features, "expert", axis=0, tiled=True)
    routed = jnp.einsum(
        "jst,td->jsd", selector, features, preferred_element_type=jnp.float32
    ).astype(jnp.bfloat16)
    projected = jnp.einsum("jwid,jsd->jwis", gate_up, routed, preferred_element_type=jnp.float32)
    gate_value = projected[:, 0]
    up_value = projected[:, 1]
    sigmoid_gate = 1.0 / (1.0 + jnp.exp(-gate_value))
    active = gate_value * sigmoid_gate
    hidden = (active * up_value).astype(jnp.bfloat16)
    grad_value = hidden_grad.astype(jnp.float32)
    gate_grad = (
        grad_value * up_value * sigmoid_gate * (1.0 + gate_value * (1.0 - sigmoid_gate))
    ).astype(jnp.bfloat16)
    up_grad = (grad_value * active).astype(jnp.bfloat16)
    grad_pair = jnp.stack([gate_grad, up_grad], axis=1)
    part = jnp.einsum(
        "jwis,jwid->jsd", grad_pair, gate_up, preferred_element_type=jnp.float32
    ).astype(jnp.bfloat16)
    partial = jnp.einsum(
        "jst,jsd->td", selector, part, preferred_element_type=jnp.float32
    ).astype(jnp.bfloat16)
    summed = lax.psum_scatter(partial, "expert", scatter_dimension=0, tiled=True)
    token_grad = lax.psum_scatter(summed, "fsdp", scatter_dimension=1, tiled=True)
    weight_grad = jnp.einsum(
        "jwis,jsd->jwid", grad_pair, routed, preferred_element_type=jnp.float32
    ).astype(jnp.bfloat16)
    return (hidden, weight_grad, token_grad)


def local(tokens, expert_ids, gate_up, hidden_grad):
    groups, fsdp = lax.axis_size("expert"), lax.axis_size("fsdp")
    local_experts = gate_up.shape[0]
    capacity = hidden_grad.shape[2] // groups
    rows, width = tokens.shape
    listing = jnp.pad(expert_ids.astype(tokens.dtype), ((0, 0), (0, 128 - expert_ids.shape[1])))
    own = jnp.concatenate([tokens, listing], axis=1).reshape(2, rows // 2, width + 128)
    full = gather_tokens(own, groups, fsdp).reshape(fsdp, groups * rows, width + 128)
    ids = full[0, :, width : width + expert_ids.shape[1]].astype(jnp.int32)
    selector = selector_of(
        ids, lax.axis_index("expert") * local_experts, local_experts, groups, capacity
    )
    hidden, weight_grad, partial = mixed(full, selector, gate_up, hidden_grad, width)
    token_grad = scatter_sum(partial.reshape(fsdp, groups, 2, rows // 2, width))
    return (hidden, weight_grad, token_grad.reshape(rows, width))


def fits(mesh, gate_up_shape, ids_shape, tokens_shape):
    groups, fsdp = mesh.shape["expert"], mesh.shape["fsdp"]
    rows = tokens_shape[0] // groups
    return (
        groups % 4 == 0
        and fsdp == 2
        and rows % 32 == 0
        and (tokens_shape[1] // fsdp) % 128 == 0
        and gate_up_shape[0] <= 256
        and ids_shape[1] <= 128
    )


def solution(mesh):
    placed = (
        P("expert", "fsdp"),
        P("expert", None),
        P("expert", None, "fsdp", None),
        P("expert", "fsdp", None),
    )
    results = (P("expert", "fsdp", None), P("expert", None, "fsdp", None), P("expert", "fsdp"))

    def run(tokens, expert_ids, gate_up, hidden_grad):
        kernels = fits(mesh, gate_up.shape, expert_ids.shape, tokens.shape)
        return jax.shard_map(
            local if kernels else local_plain,
            mesh=mesh,
            in_specs=placed,
            out_specs=results,
            check_vma=False,
        )(tokens, expert_ids, gate_up, hidden_grad)

    return run
```
